32 devices in a mesh: heads: 4 (over y, x), seq: 8 (over z, core).
Axes of the slice: x: 2, y: 2, z: 4, core: 2. Of those that a mesh axis runs over, the one named last changes fastest.
Arguments:
- hidden: bfloat16 [64, 2048], P(None, 'seq')
- w_qkv: bfloat16 [2048, 3, 2048], P('seq', None, 'heads')
- w_out: bfloat16 [2048, 2048], P('heads', 'seq'), may hold values from -0.125 to 0.125
- positions: int32 [64], replicated, may hold values from 0 to 8191
- req_blocks: int32 [64], replicated, may hold values from 1 to 64, 144 in all
- keep_list: int32 [144], P('seq'), may hold values from 0 to 1, as said below
- dest_slot: int32 [144], P('seq'), may hold values from 0 to 127, as said below
- key_cache: bfloat16 [144, 128, 2048], P('seq', None, 'heads')
- value_cache: bfloat16 [144, 128, 2048], P('seq', None, 'heads')
- fold_weight: float32 [144, 128], P('seq'), may hold values from 0.1 to 10
Outputs:
- packed_keys: bfloat16 [128, 128, 2048], P('seq', None, 'heads')
- packed_values: bfloat16 [128, 128, 2048], P('seq', None, 'heads')
- packed_request: int32 [128], P('seq')
- folded_keys: bfloat16 [144, 2048], P('seq', 'heads')
- folded_values: bfloat16 [144, 2048], P('seq', 'heads')
- attn_out: bfloat16 [64, 2048], P(None, 'seq')
The draws below stay inside these ranges and needn't reach their ends.
Inputs may be any that keep to these rules, and one draw needn't show every extreme that they name: `keep_list`: each index of seq (its 18 blocks) keeps at most 15 blocks, and some index keeps exactly that many. `dest_slot`: for a kept block: its slot among 128 packed slots, 16 to each owner (owner = slot // 16); kept blocks have distinct slots; a kept block held by index i of seq goes to owner (i + j) mod 8 for some j with 0 <= j < 4; at most 4 kept blocks of one index share an owner, and some index sends that many to one owner; some owner has all its slots filled. Entries of dropped blocks are meaningless.
All inputs are finite; a program needn't handle non-finite values.
Results may differ from the reference program's by a relative error of at most 0.0156.
The reference program's roundings to bfloat16 on the way count: a program that leaves them out, or rounds other values in their place, can miss the bound.
Values may be sent and summed in bfloat16 or wider, within the bound.
A program may use at most 128 MiB of HBM per device.

```python
import math
import jax
import jax.numpy as jnp
import numpy as np
from jax import lax

D = 2048
HEADS = 32
HDIM = 64
ROWS = 128
HOPS = 4
REQS = 64
BLK_DEV = 18
KEEP_MOST = 15
CAP = 4
SLOT_DEV = 16
BLOCKS = 144
SLOTS = 128
MOST_BLK = 64
N_SEQ = 8


def plan_blocks(key):
    keys = jax.random.split(jax.random.fold_in(key, 7), 7)
    dev_count = N_SEQ
    block_count = BLK_DEV
    most = KEEP_MOST
    hop_count = HOPS
    cap_each = CAP
    device_ids = jnp.arange(dev_count)
    counts = jax.random.randint(keys[0], (dev_count,), most // 2, most + 1)
    rotation = jax.random.randint(keys[1], (dev_count,), 0, hop_count)
    full_owner = jax.random.randint(keys[2], (), 0, dev_count)
    feeders = (full_owner - jnp.arange(hop_count)) % dev_count
    rotation = rotation.at[feeders].set(jnp.arange(hop_count))
    counts = counts.at[feeders].max((cap_each - 1) * hop_count + 1)
    full_device = jax.random.randint(keys[3], (), 0, dev_count)
    counts = jnp.where(device_ids == full_device, most, counts)
    orders = jax.vmap(lambda sub: jax.random.permutation(sub, block_count))(jax.random.split(keys[4], dev_count))
    positions_in_order = jnp.argsort(orders, axis=1)
    keep_table = (positions_in_order < counts[:, None]).astype(jnp.int32)
    kept_rank = jnp.cumsum(keep_table, axis=1) - keep_table
    hop_table = (kept_rank + rotation[:, None]) % hop_count
    owners = (device_ids[:, None] + hop_table) % dev_count
    local_index = jnp.minimum(hop_table * cap_each + kept_rank // hop_count, SLOT_DEV - 1)
    slot_perms = jax.vmap(lambda sub: jax.random.permutation(sub, SLOT_DEV))(jax.random.split(keys[5], dev_count))
    local_slot = slot_perms[owners, local_index]
    slots = owners * SLOT_DEV + local_slot
    filler = jax.random.randint(keys[6], (dev_count, block_count), 0, SLOTS)
    dest_table = jnp.where(keep_table == 1, slots, filler)
    return (keep_table.reshape(-1).astype(jnp.int32), dest_table.reshape(-1).astype(jnp.int32))


def draw_keep_list(key, part):
    return plan_blocks(key)[0]


def draw_dest_slot(key, part):
    return plan_blocks(key)[1]


def draw_w_qkv(key, part):
    keys = jax.random.split(jax.random.fold_in(key, 11), 3)
    width = HEADS * HDIM
    factor = 1.0 / math.sqrt(D)
    query_part = jax.random.truncated_normal(keys[0], -3.0, 3.0, (D, width), jnp.float32) * factor
    key_part = query_part + 0.25 * jax.random.truncated_normal(keys[1], -3.0, 3.0, (D, width), jnp.float32) * factor
    value_part = jax.random.truncated_normal(keys[2], -3.0, 3.0, (D, width), jnp.float32) * factor
    return jnp.stack([query_part, key_part, value_part], axis=1).astype(jnp.bfloat16)


def draw_hidden(key, part):
    keys = jax.random.split(key, 3)
    col_scale = 10.0 ** (jnp.arange(D, dtype=jnp.float32) / D - 0.5) * jnp.exp(jax.random.uniform(keys[0], (D,), jnp.float32, -0.3, 0.3))
    row_scale = jnp.exp(jax.random.uniform(keys[1], (REQS, 1), jnp.float32, math.log(0.3), math.log(3.0)))
    base = jax.random.normal(keys[2], (REQS, D), jnp.float32)
    return (base * row_scale * col_scale[None, :]).astype(jnp.bfloat16)


def draw_key_cache(key, part):
    keys = jax.random.split(key, 1)
    shape = (BLOCKS, ROWS, HEADS * HDIM)
    base = jax.random.normal(keys[0], shape, jnp.float32)
    return base.astype(jnp.bfloat16)


def draw_value_cache(key, part):
    keys = jax.random.split(key, 2)
    shape = (BLOCKS, ROWS, HEADS * HDIM)
    offsets = jax.random.uniform(keys[0], (BLOCKS, 1, HEADS * HDIM), jnp.float32, -2.0, 2.0)
    noise = 0.5 * jax.random.normal(keys[1], shape, jnp.float32)
    return (offsets + noise).astype(jnp.bfloat16)


def touch_ends(array, key, smallest, high):
    extent = array.shape
    index_at = [jax.random.randint(jax.random.fold_in(key, axis), (), 0, extent[axis]) for axis in range(len(extent))]
    array = array.at[tuple(index_at)].set(smallest)
    longest = extent.index(max(extent))
    index_at[longest] = (index_at[longest] + 1) % extent[longest]
    return array.at[tuple(index_at)].set(high)


def block_scale(stream_key, shape, shards, smallest, high):
    def one(dim, shards_of):
        steps = jax.random.uniform(jax.random.fold_in(jax.random.fold_in(stream_key, 6), dim), (shards_of,), jnp.float32, smallest / len(shards), high / len(shards))
        return jnp.repeat(jnp.exp(steps), shape[dim] // shards_of).reshape((-1,) + (1,) * (len(shape) - dim - 1))

    factor_of = one(*shards[0])
    for cut in shards[1:]:
        factor_of = factor_of * one(*cut)
    return factor_of


def length_profile(amount, total, most, skew):
    loads = [(1 << 20) // math.isqrt(rank ** skew) + 1 for rank in range(2, amount + 1)]
    rest, holding = total - most - (amount - 1), [1] * (amount - 1)
    while rest > 0:
        movable = [i for i in range(amount - 1) if holding[i] < most]
        whole, budget = sum([loads[i] for i in movable]), rest
        for i in movable:
            extra = min(most - holding[i], max(1, budget * loads[i] // whole), rest)
            holding[i] = holding[i] + extra
            rest = rest - extra
    return np.array([most] + holding)


def uneven(stream_key, count, total, bound, lean):
    if count == 2:
        one = jax.random.randint(stream_key, (), max(1, total - bound), min(bound, total - 1) + 1)
        return jnp.stack([one, total - one])
    tallies = jnp.asarray(length_profile(count, total, bound, lean), jnp.int32)
    couples = (count - 1) // 2
    giver, receiver = tallies[1:1 + 2 * couples:2], tallies[2:2 + 2 * couples:2]
    room = jnp.minimum(giver - 1, bound - receiver)
    shifted = jax.random.randint(jax.random.fold_in(stream_key, 1), (couples,), 0, 1 << 20) % (room + 1)
    tallies = tallies.at[1:1 + 2 * couples:2].set(giver - shifted).at[2:2 + 2 * couples:2].set(receiver + shifted)
    return tallies[jax.random.permutation(jax.random.fold_in(stream_key, 2), count)]


def normal_values(own_key, dims, spread, most, cuts=(), kind=jnp.bfloat16):
    result = spread * jax.random.normal(own_key, dims, jnp.float32)
    if cuts:
        result = result * block_scale(own_key, dims, cuts, -0.22, 0.18)
    return jnp.clip(result, -most, most).astype(kind)


def setup_inputs(seed: int = 0) -> dict:
    seeds = jax.random.split(jax.random.key(seed), 11)
    return {
        "hidden": draw_hidden(jax.random.fold_in(seeds[10], 71), 0),
        "w_qkv": draw_w_qkv(jax.random.fold_in(seeds[10], 71), 0),
        "w_out": normal_values(seeds[2], (HEADS * HDIM, D), (HEADS * HDIM) ** -0.5, 0.125, ((0, 4), (1, 8))),
        "positions": touch_ends(jax.random.randint(seeds[3], (REQS,), 0, 8192), jax.random.fold_in(seeds[3], 1), 0, 8191).astype(jnp.int32),
        "req_blocks": uneven(seeds[4], REQS, BLOCKS, MOST_BLK, 2).astype(jnp.int32),
        "keep_list": draw_keep_list(jax.random.fold_in(seeds[10], 71), 0),
        "dest_slot": draw_dest_slot(jax.random.fold_in(seeds[10], 71), 0),
        "key_cache": draw_key_cache(jax.random.fold_in(seeds[10], 71), 0),
        "value_cache": draw_value_cache(jax.random.fold_in(seeds[10], 71), 0),
        "fold_weight": jnp.clip(jnp.exp(math.log(10.0) - 4.6051702 * jax.random.uniform(seeds[9], (BLOCKS, ROWS), jnp.float32) ** block_scale(seeds[9], (BLOCKS, ROWS), ((0, 8),), -0.2, 0.2)), 0.1, 10.0),
    }


ROPE_BASE = 130000.0
NORM_EPSILON = 1e-05

def rotate_half(values, cos_table, sin_table):
    half = values.shape[-1] // 2
    lower = values[..., :half]
    upper = values[..., half:]
    return jnp.concatenate([lower * cos_table - upper * sin_table, upper * cos_table + lower * sin_table], axis=-1)

def rope_tables(positions, head_size):
    half = head_size // 2
    freqs = ROPE_BASE ** (-(2.0 * jnp.arange(half, dtype=jnp.float32)) / head_size)
    angles = positions.astype(jnp.float32)[:, None] * freqs[None, :]
    return (jnp.cos(angles)[:, None, :], jnp.sin(angles)[:, None, :])

def fold_block(inputs):
    weights, keys_block, values_block = inputs
    weight_sum = jnp.sum(weights)
    fold_keys = jnp.dot(weights, keys_block.astype(jnp.float32), precision=lax.Precision.HIGHEST) / weight_sum
    fold_values = jnp.dot(weights, values_block.astype(jnp.float32), precision=lax.Precision.HIGHEST) / weight_sum
    return (fold_keys, fold_values)

def reference(hidden, w_qkv, w_out, positions, req_blocks, keep_list, dest_slot, key_cache, value_cache, fold_weight):
    width = HEADS * HDIM
    widened = hidden.astype(jnp.float32)
    mean_square = lax.optimization_barrier(jnp.mean(widened * widened, axis=1, keepdims=True))
    normed = (widened * lax.rsqrt(mean_square + NORM_EPSILON)).astype(jnp.bfloat16)
    proj_all = jnp.dot(normed, w_qkv.reshape(D, 3 * width), preferred_element_type=jnp.float32)
    proj_all = proj_all.reshape(REQS, 3, HEADS, HDIM)
    cos_table, sin_table = rope_tables(positions, HDIM)
    queries = rotate_half(proj_all[:, 0], cos_table, sin_table).astype(jnp.bfloat16)
    new_keys = rotate_half(proj_all[:, 1], cos_table, sin_table).astype(jnp.bfloat16)
    new_values = proj_all[:, 2].astype(jnp.bfloat16)
    req_ends = jnp.cumsum(req_blocks)
    block_ids = jnp.arange(BLOCKS, dtype=jnp.int32)
    blk_req = lax.optimization_barrier(jnp.sum((block_ids[:, None] >= req_ends[None, :]).astype(jnp.int32), axis=1)).astype(jnp.int32)
    is_kept = keep_list == 1
    slot_index = jnp.where(is_kept, dest_slot, SLOTS).astype(jnp.int32)
    packed_keys = jnp.zeros((SLOTS + 1, ROWS, width), jnp.bfloat16).at[slot_index].set(key_cache)[:SLOTS]
    packed_values = jnp.zeros((SLOTS + 1, ROWS, width), jnp.bfloat16).at[slot_index].set(value_cache)[:SLOTS]
    packed_request = jnp.full((SLOTS + 1,), -1, jnp.int32).at[slot_index].set(blk_req)[:SLOTS]
    fold_keys, fold_values = lax.map(fold_block, (fold_weight, key_cache, value_cache))
    folded_keys = jnp.where(is_kept[:, None], 0.0, fold_keys).astype(jnp.bfloat16)
    folded_values = jnp.where(is_kept[:, None], 0.0, fold_values).astype(jnp.bfloat16)
    row_req = jnp.concatenate([jnp.repeat(packed_request, ROWS), jnp.where(is_kept, -1, blk_req).astype(jnp.int32), jnp.arange(REQS, dtype=jnp.int32)])
    segment = jnp.where(row_req >= 0, row_req, REQS).astype(jnp.int32)
    bias = jnp.concatenate([jnp.zeros((SLOTS * ROWS,), jnp.float32), jnp.full((BLOCKS,), math.log(ROWS), jnp.float32), jnp.zeros((REQS,), jnp.float32)])
    all_keys = jnp.concatenate([packed_keys.reshape(SLOTS * ROWS, HEADS, HDIM), folded_keys.reshape(BLOCKS, HEADS, HDIM), new_keys], axis=0)
    all_values = jnp.concatenate([packed_values.reshape(SLOTS * ROWS, HEADS, HDIM), folded_values.reshape(BLOCKS, HEADS, HDIM), new_values], axis=0)
    pick_rows = jnp.minimum(segment, REQS - 1)

    def head_mix(inputs):
        query_head, keys_head, values_head = inputs
        gathered = query_head[pick_rows]
        scores = lax.optimization_barrier(jnp.sum(gathered.astype(jnp.float32) * keys_head.astype(jnp.float32), axis=1)) * 0.125 + bias
        tops = jax.ops.segment_max(scores, segment, REQS + 1)
        expo = jnp.exp(scores - tops[segment])
        sums = jax.ops.segment_sum(expo, segment, REQS + 1)
        probs = lax.optimization_barrier(expo.astype(jnp.bfloat16)).astype(jnp.float32)
        weighted = jax.ops.segment_sum(probs[:, None] * values_head.astype(jnp.float32), segment, REQS + 1)
        return weighted[:REQS] / sums[:REQS, None]
    mixture = lax.map(head_mix, (jnp.transpose(queries, (1, 0, 2)), jnp.transpose(all_keys, (1, 0, 2)), jnp.transpose(all_values, (1, 0, 2))))
    mixed = jnp.transpose(mixture, (1, 0, 2)).reshape(REQS, width).astype(jnp.bfloat16)
    attn_out = jnp.dot(mixed, w_out, preferred_element_type=jnp.float32).astype(jnp.bfloat16)
    return (packed_keys, packed_values, packed_request, folded_keys, folded_values, attn_out)
```

```python
import functools
import math

import jax
import jax.numpy as jnp
from jax import lax
from jax.experimental import pallas as pl
from jax.experimental.pallas import tpu as pltpu
from jax.sharding import PartitionSpec as P

D = 2048
HDIM = 64
ROWS = 128
HOPS = 4
CAP = 4
SLOT_DEV = 16

ROPE_BASE = 130000.0
NORM_EPSILON = 1e-05
MASKED_SCORE = -1e30
MESH = pl.DeviceIdType.MESH
F32 = jnp.float32
BF16 = jnp.bfloat16
HIGHEST = lax.Precision.HIGHEST


def pack_kernel(seq_count, keep, dest, req, keys, values, send_k, send_v, meta, count, sem):
    me = lax.axis_index("seq")
    n_blocks = keep.shape[0]
    for hop in range(HOPS):
        count[hop] = 0
        for place in range(CAP):
            meta[hop, 0, place] = -1
            meta[hop, 1, place] = -1
            meta[hop, 2, place] = 0

    def moves(g, hop, place):
        at = (hop - 1) * CAP + place
        return (
            pltpu.make_async_copy(keys.at[g], send_k.at[at], sem),
            pltpu.make_async_copy(values.at[g], send_v.at[at], sem),
        )

    def step(g, sent):
        kept = keep[g] == 1
        slot = dest[g]
        hop = lax.rem(slot // SLOT_DEV - me + seq_count, seq_count)
        hop = jnp.where(kept, hop, 0)
        place = count[hop]

        @pl.when(kept)
        def _():
            count[hop] = place + 1
            meta[hop, 0, place] = lax.rem(slot, SLOT_DEV)
            meta[hop, 1, place] = req[g]
            meta[hop, 2, place] = g

        away = kept & (hop > 0)

        @pl.when(away)
        def _():
            for move in moves(g, hop, place):
                move.start()

        return sent + away.astype(jnp.int32)

    sent = lax.fori_loop(0, n_blocks, step, jnp.int32(0))

    def drain(_, carry):
        for move in moves(0, 1, 0):
            move.wait()
        return carry

    lax.fori_loop(0, sent, drain, 0)


def place_kernel(meta, keys, values, recv_k, recv_v, out_k, out_v, out_req, zeros, sem):
    zeros[...] = jnp.zeros_like(zeros)
    for slot in range(SLOT_DEV):
        out_req[slot] = -1
    for hop in range(HOPS):
        for place in range(CAP):
            slot = meta[hop, 0, place]

            @pl.when(slot >= 0)
            def _():
                out_req[slot] = meta[hop, 1, place]
                if hop == 0:
                    g = meta[0, 2, place]
                    from_k, from_v = keys.at[g], values.at[g]
                else:
                    at = (hop - 1) * CAP + place
                    from_k, from_v = recv_k.at[at], recv_v.at[at]
                pltpu.make_async_copy(from_k, out_k.at[slot], sem).start()
                pltpu.make_async_copy(from_v, out_v.at[slot], sem).start()

    for slot in range(SLOT_DEV):

        @pl.when(out_req[slot] < 0)
        def _():
            pltpu.make_async_copy(zeros, out_k.at[slot], sem).start()
            pltpu.make_async_copy(zeros, out_v.at[slot], sem).start()

    for slot in range(SLOT_DEV):
        pltpu.make_async_copy(zeros, out_k.at[slot], sem).wait()
        pltpu.make_async_copy(zeros, out_v.at[slot], sem).wait()


def rows_of(ref, lead, each):
    if each % 8 == 0:
        return ref[...].reshape(lead * each, ref.shape[-1])
    return jnp.concatenate([ref[d] for d in range(lead)], axis=0)


def main_kernel(
    n,
    n_heads,
    hidden,
    w_qkv,
    w_out,
    cos,
    sin,
    onehot,
    onehot_t,
    first_t,
    same,
    keep,
    fold_w,
    meta,
    keys,
    values,
    send_k,
    send_v,
    recv_k,
    recv_v,
    recv_meta,
    out_fk,
    out_fv,
    out_attn,
    kbuf,
    vbuf,
    fk,
    fv,
    tops,
    sums,
    accs,
    sq_buf,
    part_send,
    part_recv,
    q_all,
    mix_send,
    mix_recv,
    mixed_all,
    head_buf,
    load_sem,
    bulk_sem,
    meta_sem,
    seq_sem,
    head_sem,
):
    me = lax.axis_index("seq")
    my_head = lax.axis_index("heads")
    requests = hidden.shape[0]
    each = requests // n
    n_blocks = kbuf.shape[0]
    width = kbuf.shape[2]
    heads_here = width // HDIM

    load_k = pltpu.make_async_copy(keys, kbuf, load_sem.at[0])
    load_v = pltpu.make_async_copy(values, vbuf, load_sem.at[1])
    load_k.start()
    load_v.start()

    barrier = pltpu.get_barrier_semaphore()

    def peers(body):
        if n <= 8:
            for k in range(1, n):
                body(k, lax.rem(me + k, n))
        else:

            def step(k, carry):
                body(k, lax.rem(me + k, n))
                return carry

            lax.fori_loop(1, n, step, 0)

    peers(
        lambda k, d: pl.semaphore_signal(barrier, inc=1, device_id={"seq": d}, device_id_type=MESH)
    )
    for k in range(1, n_heads):
        pl.semaphore_signal(
            barrier,
            inc=1,
            device_id={"heads": lax.rem(my_head + k, n_heads)},
            device_id_type=MESH,
        )

    wide = hidden[...].astype(F32)
    col = jnp.sum(wide * wide, axis=1, keepdims=True)
    eye = lax.broadcasted_iota(jnp.int32, (requests, 128), 0) == lax.broadcasted_iota(
        jnp.int32, (requests, 128), 1
    )
    row = jnp.sum(jnp.where(eye, col, 0.0), axis=0, keepdims=True)
    sq_buf[me] = jnp.broadcast_to(row, (8, 128))

    pl.semaphore_wait(barrier, n - 1 + n_heads - 1)

    def exchange(stage, source, target):
        def copy(k, d):
            return pltpu.make_async_remote_copy(
                src_ref=source(d),
                dst_ref=target.at[me],
                send_sem=seq_sem.at[2 * stage, k],
                recv_sem=seq_sem.at[2 * stage + 1, k],
                device_id={"seq": d},
                device_id_type=MESH,
            )

        return (
            lambda: peers(lambda k, d: copy(k, d).start()),
            lambda: peers(lambda k, d: copy(k, d).wait_recv()),
            lambda: peers(lambda k, d: copy(k, d).wait_send()),
        )

    bulk = []
    for hop in range(1, HOPS):
        for which, (source, target) in enumerate(((send_k, recv_k), (send_v, recv_v))):
            at = pl.ds((hop - 1) * CAP, CAP)
            bulk.append(
                pltpu.make_async_remote_copy(
                    src_ref=source.at[at],
                    dst_ref=target.at[at],
                    send_sem=bulk_sem.at[0, 2 * hop - 2 + which],
                    recv_sem=bulk_sem.at[1, 2 * hop - 2 + which],
                    device_id={"seq": lax.rem(me + hop, n)},
                    device_id_type=MESH,
                )
            )
    metas = [
        pltpu.make_async_remote_copy(
            src_ref=meta.at[hop],
            dst_ref=recv_meta.at[hop],
            send_sem=meta_sem.at[0, hop],
            recv_sem=meta_sem.at[1, hop],
            device_id={"seq": lax.rem(me + hop, n)},
            device_id_type=MESH,
        )
        for hop in range(1, HOPS)
    ]

    sq_start, sq_wait, sq_done = exchange(0, lambda d: sq_buf.at[me], sq_buf)
    sq_start()
    for copy in metas:
        copy.start()
    for copy in bulk:
        copy.start()
    recv_meta[0] = meta[0]

    load_k.wait()
    load_v.wait()
    line = lax.broadcasted_iota(jnp.int32, (8, ROWS), 0)

    def fold(g, carry):
        weights = fold_w[pl.ds(g, 1), :]
        high = weights.astype(BF16).astype(F32)
        rest = weights - high
        middle = rest.astype(BF16).astype(F32)
        low = rest - middle
        stacked = jnp.where(
            line == 0, high, jnp.where(line == 1, middle, jnp.where(line == 2, low, 0.0))
        ).astype(BF16)
        total = jnp.sum(weights, axis=1, keepdims=True)
        folded_k = jnp.dot(stacked, kbuf[g], preferred_element_type=F32)
        folded_v = jnp.dot(stacked, vbuf[g], preferred_element_type=F32)
        fk[pl.ds(g, 1), :] = (
            (jnp.sum(folded_k, axis=0, keepdims=True) / total).astype(BF16).astype(F32)
        )
        fv[pl.ds(g, 1), :] = (
            (jnp.sum(folded_v, axis=0, keepdims=True) / total).astype(BF16).astype(F32)
        )
        return carry

    lax.fori_loop(0, n_blocks, fold, 0)
    out_fk[...] = jnp.where(keep[...] > 0.5, 0.0, fk[...]).astype(BF16)
    out_fv[...] = jnp.where(keep[...] > 0.5, 0.0, fv[...]).astype(BF16)

    sq_wait()
    row = jnp.sum(sq_buf[...], axis=0)[0:1, :]
    col = jnp.sum(jnp.where(eye, row, 0.0), axis=1, keepdims=True)
    normed = (wide * lax.rsqrt(col / D + NORM_EPSILON)).astype(BF16)
    for part in range(3):
        product = jnp.dot(normed, w_qkv[part], preferred_element_type=F32)
        for d in range(n):
            part_send[d, part] = product[d * each : (d + 1) * each]
    part_start, part_wait, part_done = exchange(1, lambda d: part_send.at[d], part_recv)
    part_start()
    part_recv[me] = part_send[me]
    part_wait()
    proj = [jnp.sum(part_recv[:, part], axis=0) for part in range(3)]

    lane = lax.broadcasted_iota(jnp.int32, (each, width), 1)
    lower = lax.rem(lane, HDIM) < HDIM // 2
    my_cos, my_sin = cos[me], sin[me]

    def rotated(x):
        ahead = jnp.concatenate([x[:, HDIM // 2 :], x[:, : HDIM // 2]], axis=1)
        behind = jnp.concatenate([x[:, -(HDIM // 2) :], x[:, : -(HDIM // 2)]], axis=1)
        return (x * my_cos + jnp.where(lower, ahead, behind) * my_sin).astype(BF16).astype(F32)

    query = rotated(proj[0])
    new_key = rotated(proj[1])
    new_value = proj[2].astype(BF16).astype(F32)
    q_all[me] = query
    q_start, q_wait, q_done = exchange(2, lambda d: q_all.at[me], q_all)
    q_start()
    q_wait()

    q_rows = rows_of(q_all, n, each).astype(BF16)
    accs[...] = jnp.dot(onehot[...].astype(BF16), q_rows, preferred_element_type=F32)
    head_mask = (
        lax.broadcasted_iota(jnp.int32, (heads_here, width), 1) // HDIM
        == lax.broadcasted_iota(jnp.int32, (heads_here, width), 0)
    )

    def spread(column):
        return jnp.sum(jnp.where(head_mask, column, 0.0), axis=0, keepdims=True)

    def attend(g, carry):
        query_g = jnp.where(head_mask, accs[pl.ds(g, 1), :], 0.0)
        scores = (
            lax.dot_general(
                query_g.astype(BF16),
                kbuf[g],
                (((1,), (1,)), ((), ())),
                preferred_element_type=F32,
            )
            * 0.125
        )
        top = jnp.max(scores, axis=1, keepdims=True)
        expo = jnp.exp(scores - top)
        total = jnp.sum(expo, axis=1, keepdims=True)
        mix = jnp.dot(expo.astype(BF16), vbuf[g], preferred_element_type=F32)
        mix = jnp.sum(jnp.where(head_mask, mix, 0.0), axis=0, keepdims=True)
        folded_score = jnp.sum(
            query_g * fk[pl.ds(g, 1), :], axis=1, keepdims=True
        ) * 0.125 + math.log(ROWS)
        kept = keep[pl.ds(g, 1), :] > 0.5
        tops[pl.ds(g, 1), :] = jnp.where(kept, spread(top), spread(folded_score))
        sums[pl.ds(g, 1), :] = jnp.where(kept, spread(total), 1.0)
        accs[pl.ds(g, 1), :] = jnp.where(kept, mix, fv[pl.ds(g, 1), :])
        return carry

    lax.fori_loop(0, n_blocks, attend, 0)
    block_tops = tops[...]
    req_top = jnp.full_like(block_tops, MASKED_SCORE)
    for g in range(n_blocks):
        req_top = jnp.maximum(
            req_top, jnp.where(same[:, g : g + 1] > 0.5, block_tops[g : g + 1], MASKED_SCORE)
        )
    factor = jnp.exp(block_tops - req_top)

    def by_request(table, array):
        return jnp.dot(table[...], array, precision=HIGHEST, preferred_element_type=F32)

    present = jnp.sum(first_t[...], axis=1, keepdims=True)
    top_rows = jnp.where(present > 0.5, by_request(first_t, req_top), MASKED_SCORE)
    sum_rows = by_request(onehot_t, sums[...] * factor)
    acc_rows = by_request(onehot_t, accs[...] * factor)
    for part, rows in enumerate((top_rows, sum_rows, acc_rows)):
        for d in range(n):
            mix_send[d, part] = rows[d * each : (d + 1) * each]
    mix_start, mix_wait, mix_done = exchange(3, lambda d: mix_send.at[d], mix_recv)
    mix_start()
    mix_recv[me] = mix_send[me]

    block_diag = (
        lax.broadcasted_iota(jnp.int32, (width, width), 0) // HDIM
        == lax.broadcasted_iota(jnp.int32, (width, width), 1) // HDIM
    ).astype(F32)
    own_score = (
        jnp.dot(query * new_key, block_diag, precision=HIGHEST, preferred_element_type=F32) * 0.125
    )
    mix_wait()
    all_tops = mix_recv[:, 0]
    final_top = jnp.maximum(jnp.max(all_tops, axis=0), own_score)
    scale = jnp.exp(all_tops - final_top[None])
    own_expo = jnp.exp(own_score - final_top)
    totals = jnp.sum(mix_recv[:, 1] * scale, axis=0) + own_expo
    mixture = (
        jnp.sum(mix_recv[:, 2] * scale, axis=0) + own_expo.astype(BF16).astype(F32) * new_value
    )
    mixed_all[me] = (mixture / totals).astype(BF16).astype(F32)
    mixed_start, mixed_wait, mixed_done = exchange(4, lambda d: mixed_all.at[me], mixed_all)
    mixed_start()
    mixed_wait()

    mixed_rows = rows_of(mixed_all, n, each).astype(BF16)
    head_buf[my_head] = jnp.dot(mixed_rows, w_out[...], preferred_element_type=F32)
    head_copies = [
        pltpu.make_async_remote_copy(
            src_ref=head_buf.at[my_head],
            dst_ref=head_buf.at[my_head],
            send_sem=head_sem.at[0, k],
            recv_sem=head_sem.at[1, k],
            device_id={"heads": lax.rem(my_head + k, n_heads)},
            device_id_type=MESH,
        )
        for k in range(1, n_heads)
    ]
    for copy in head_copies:
        copy.start()
    for copy in head_copies:
        copy.wait_recv()
    total = head_buf[0]
    for h in range(1, n_heads):
        total = total + head_buf[h]
    out_attn[...] = total.astype(BF16)

    for done in (sq_done, part_done, q_done, mix_done, mixed_done):
        done()
    for copy in head_copies:
        copy.wait_send()
    for copy in metas + bulk:
        copy.wait()


def shards(
    n,
    n_heads,
    hidden,
    w_qkv,
    w_out,
    positions,
    req_blocks,
    keep_list,
    dest_slot,
    key_cache,
    value_cache,
    fold_weight,
):
    requests = hidden.shape[0]
    n_blocks, row_count, width = key_cache.shape
    me = lax.axis_index("seq")
    each = requests // n
    moved = (HOPS - 1) * CAP

    ids = jnp.arange(requests, dtype=jnp.int32)
    ends = jnp.sum(jnp.where(ids[None, :] <= ids[:, None], req_blocks[None, :], 0), axis=1)
    block_ids = jnp.arange(n_blocks, dtype=jnp.int32)
    global_ids = me * n_blocks + block_ids
    blk_req = jnp.sum((global_ids[:, None] >= ends[None, :]).astype(jnp.int32), axis=1)
    onehot = (blk_req[:, None] == ids[None, :]).astype(F32)
    onehot_t = (blk_req[None, :] == ids[:, None]).astype(F32)
    same_bool = blk_req[:, None] == blk_req[None, :]
    same = same_bool.astype(F32)
    has_earlier = jnp.any(same_bool & (block_ids[None, :] < block_ids[:, None]), axis=1)
    first_t = jnp.where(has_earlier[None, :], 0.0, onehot_t)
    keep_rows = jnp.broadcast_to((keep_list == 1).astype(F32)[:, None], (n_blocks, width))

    half = HDIM // 2
    freqs = ROPE_BASE ** (-(2.0 * jnp.arange(half, dtype=F32)) / HDIM)
    angles = positions.astype(F32)[:, None] * freqs[None, :]
    cos_half, sin_half = jnp.cos(angles), jnp.sin(angles)
    copies = width // HDIM
    cos = jnp.tile(jnp.concatenate([cos_half, cos_half], axis=1), (1, copies))
    sin = jnp.tile(jnp.concatenate([-sin_half, sin_half], axis=1), (1, copies))
    cos = cos.reshape(n, each, width)
    sin = sin.reshape(n, each, width)

    smem = pl.BlockSpec(memory_space=pltpu.SMEM)
    vmem = pl.BlockSpec(memory_space=pltpu.VMEM)
    hbm = pl.BlockSpec(memory_space=pl.ANY)
    moved_shape = jax.ShapeDtypeStruct((moved, row_count, width), BF16)
    meta_shape = jax.ShapeDtypeStruct((HOPS, 8, 128), jnp.int32)
    folded_shape = jax.ShapeDtypeStruct((n_blocks, width), BF16)

    send_k, send_v, meta = pl.pallas_call(
        functools.partial(pack_kernel, n),
        out_shape=(moved_shape, moved_shape, meta_shape),
        in_specs=[smem, smem, smem, hbm, hbm],
        out_specs=(hbm, hbm, smem),
        scratch_shapes=[pltpu.SMEM((HOPS,), jnp.int32), pltpu.SemaphoreType.DMA],
        name="pack_blocks",
    )(keep_list, dest_slot, blk_req, key_cache, value_cache)

    block_rows = pltpu.VMEM((n_blocks, width), F32)
    request_rows = pltpu.VMEM((n, each, width), F32)
    three_parts = pltpu.VMEM((n, 3, each, width), F32)
    recv_k, recv_v, recv_meta, folded_keys, folded_values, attn_out = pl.pallas_call(
        functools.partial(main_kernel, n, n_heads),
        out_shape=(
            moved_shape,
            moved_shape,
            meta_shape,
            folded_shape,
            folded_shape,
            jax.ShapeDtypeStruct((requests, w_out.shape[1]), BF16),
        ),
        in_specs=[vmem] * 12 + [hbm] * 4,
        out_specs=(hbm, hbm, vmem, vmem, vmem, vmem),
        scratch_shapes=[
            pltpu.VMEM((n_blocks, row_count, width), BF16),
            pltpu.VMEM((n_blocks, row_count, width), BF16),
            block_rows,
            block_rows,
            block_rows,
            block_rows,
            block_rows,
            pltpu.VMEM((n, 8, 128), F32),
            three_parts,
            three_parts,
            request_rows,
            three_parts,
            three_parts,
            request_rows,
            pltpu.VMEM((n_heads, requests, w_out.shape[1]), F32),
            pltpu.SemaphoreType.DMA((2,)),
            pltpu.SemaphoreType.DMA((2, 2 * (HOPS - 1))),
            pltpu.SemaphoreType.DMA((2, HOPS)),
            pltpu.SemaphoreType.DMA((10, n)),
            pltpu.SemaphoreType.DMA((2, n_heads)),
        ],
        compiler_params=pltpu.CompilerParams(
            collective_id=0, has_side_effects=True, vmem_limit_bytes=48 * 2**20
        ),
        name="decode_and_move",
    )(
        hidden,
        jnp.transpose(w_qkv, (1, 0, 2)),
        w_out,
        cos,
        sin,
        onehot,
        onehot_t,
        first_t,
        same,
        keep_rows,
        fold_weight,
        meta,
        key_cache,
        value_cache,
        send_k,
        send_v,
    )

    packed_shape = jax.ShapeDtypeStruct((SLOT_DEV, row_count, width), BF16)
    packed_keys, packed_values, packed_request = pl.pallas_call(
        place_kernel,
        out_shape=(packed_shape, packed_shape, jax.ShapeDtypeStruct((SLOT_DEV,), jnp.int32)),
        in_specs=[smem, hbm, hbm, hbm, hbm],
        out_specs=(hbm, hbm, smem),
        scratch_shapes=[pltpu.VMEM((row_count, width), BF16), pltpu.SemaphoreType.DMA],
        name="place_blocks",
    )(recv_meta, key_cache, value_cache, recv_k, recv_v)
    return (packed_keys, packed_values, packed_request, folded_keys, folded_values, attn_out)


def solution(mesh):
    return jax.shard_map(
        functools.partial(shards, mesh.shape["seq"], mesh.shape["heads"]),
        mesh=mesh,
        in_specs=(
            P(None, "seq"),
            P("seq", None, "heads"),
            P("heads", "seq"),
            P(),
            P(),
            P("seq"),
            P("seq"),
            P("seq", None, "heads"),
            P("seq", None, "heads"),
            P("seq", None),
        ),
        out_specs=(
            P("seq", None, "heads"),
            P("seq", None, "heads"),
            P("seq"),
            P("seq", "heads"),
            P("seq", "heads"),
            P(None, "seq"),
        ),
        check_vma=False,
    )
```

```python
import functools
import math

import jax
import jax.numpy as jnp
from jax import lax
from jax.experimental import pallas as pl
from jax.experimental.pallas import tpu as pltpu
from jax.sharding import PartitionSpec as P

D = 2048
HDIM = 64
ROWS = 128
HOPS = 4
CAP = 4
SLOT_DEV = 16
TURNS = (6, 3, 0, 3, 0, 12)
GROUP = 6

ROPE_BASE = 130000.0
NORM_EPSILON = 1e-05
MASKED_SCORE = -1e30
MESH = pl.DeviceIdType.MESH
F32 = jnp.float32
BF16 = jnp.bfloat16
HIGHEST = lax.Precision.HIGHEST


def pack_kernel(seq_count, keep, dest, req, keys, values, own_k, own_v, send_k, send_v, meta, count):
    me = lax.axis_index("seq")
    n_blocks = keep.shape[0]
    for hop in range(HOPS):
        count[hop] = 0
        for place in range(CAP):
            meta[hop, 0, place] = -1
            meta[hop, 1, place] = -1

    def step(g, carry):
        slot = dest[g]
        hop = lax.rem(slot // SLOT_DEV - me + seq_count, seq_count)
        kept = keep[g] == 1

        @pl.when(kept)
        def _():
            place = count[hop]
            count[hop] = place + 1
            meta[hop, 0, place] = lax.rem(slot, SLOT_DEV)
            meta[hop, 1, place] = req[g]

            @pl.when(hop == 0)
            def _():
                own_k[place] = keys[g]
                own_v[place] = values[g]

            @pl.when(hop > 0)
            def _():
                at = (hop - 1) * CAP + place
                send_k[at] = keys[g]
                send_v[at] = values[g]

        return carry

    lax.fori_loop(0, n_blocks, step, 0)


def place_kernel(meta, own_k, own_v, recv_k, recv_v, out_k, out_v, out_req, zeros, sem):
    zeros[...] = jnp.zeros_like(zeros)
    for slot in range(SLOT_DEV):
        out_req[slot] = -1
    for hop in range(HOPS):
        for place in range(CAP):
            slot = meta[hop, 0, place]
            at = (hop - 1) * CAP + place
            from_k = own_k.at[place] if hop == 0 else recv_k.at[at]
            from_v = own_v.at[place] if hop == 0 else recv_v.at[at]

            @pl.when(slot >= 0)
            def _():
                out_req[slot] = meta[hop, 1, place]
                pltpu.make_async_copy(from_k, out_k.at[slot], sem).start()
                pltpu.make_async_copy(from_v, out_v.at[slot], sem).start()

    for slot in range(SLOT_DEV):

        @pl.when(out_req[slot] < 0)
        def _():
            pltpu.make_async_copy(zeros, out_k.at[slot], sem).start()
            pltpu.make_async_copy(zeros, out_v.at[slot], sem).start()

    for slot in range(SLOT_DEV):
        pltpu.make_async_copy(zeros, out_k.at[slot], sem).wait()
        pltpu.make_async_copy(zeros, out_v.at[slot], sem).wait()


def rows_of(ref, lead, each):
    if each % 8 == 0:
        return ref[...].reshape(lead * each, ref.shape[-1])
    return jnp.concatenate([ref[d] for d in range(lead)], axis=0)


def main_kernel(
    n,
    n_heads,
    hidden,
    w_qkv,
    w_out,
    cos,
    sin,
    onehot,
    onehot_t,
    first_t,
    same,
    keep,
    fold_w,
    meta,
    keys,
    values,
    send_k,
    send_v,
    recv_k,
    recv_v,
    recv_meta,
    out_fk,
    out_fv,
    out_attn,
    kbuf,
    vbuf,
    fk,
    fv,
    tops,
    sums,
    accs,
    sq_buf,
    part_send,
    part_recv,
    q_all,
    mix_send,
    mix_recv,
    mixed_all,
    head_buf,
    load_sem,
    bulk_sem,
    meta_sem,
    seq_sem,
    head_sem,
):
    me = lax.axis_index("seq")
    my_head = lax.axis_index("heads")
    requests = hidden.shape[0]
    each = requests // n
    n_blocks = kbuf.shape[0]
    width = kbuf.shape[2]
    heads_here = width // HDIM

    load_k = pltpu.make_async_copy(keys, kbuf, load_sem.at[0])
    load_v = pltpu.make_async_copy(values, vbuf, load_sem.at[1])
    load_k.start()
    load_v.start()

    barrier = pltpu.get_barrier_semaphore()

    def peers(body):
        if n <= 8:
            for k in range(1, n):
                body(k, lax.rem(me + k, n))
        else:

            def step(k, carry):
                body(k, lax.rem(me + k, n))
                return carry

            lax.fori_loop(1, n, step, 0)

    peers(
        lambda k, d: pl.semaphore_signal(barrier, inc=1, device_id={"seq": d}, device_id_type=MESH)
    )
    for k in range(1, n_heads):
        pl.semaphore_signal(
            barrier,
            inc=1,
            device_id={"heads": lax.rem(my_head + k, n_heads)},
            device_id_type=MESH,
        )

    wide = hidden[...].astype(F32)
    col = jnp.sum(wide * wide, axis=1, keepdims=True)
    eye = lax.broadcasted_iota(jnp.int32, (requests, 128), 0) == lax.broadcasted_iota(
        jnp.int32, (requests, 128), 1
    )
    row = jnp.sum(jnp.where(eye, col, 0.0), axis=0, keepdims=True)
    sq_buf[me] = jnp.broadcast_to(row, (8, 128))

    pl.semaphore_wait(barrier, n - 1 + n_heads - 1)

    def exchange(stage, source, target):
        def copy(k, d):
            return pltpu.make_async_remote_copy(
                src_ref=source(d),
                dst_ref=target.at[me],
                send_sem=seq_sem.at[2 * stage, k],
                recv_sem=seq_sem.at[2 * stage + 1, k],
                device_id={"seq": d},
                device_id_type=MESH,
            )

        return (
            lambda: peers(lambda k, d: copy(k, d).start()),
            lambda: peers(lambda k, d: copy(k, d).wait_recv()),
            lambda: peers(lambda k, d: copy(k, d).wait_send()),
        )

    def block_copies(pair):
        hop, place = HOPS - 1 - pair // CAP, pair % CAP
        at = (hop - 1) * CAP + place
        return [
            pltpu.make_async_remote_copy(
                src_ref=source.at[at],
                dst_ref=target.at[at],
                send_sem=bulk_sem.at[which, at],
                recv_sem=bulk_sem.at[which + 2, at],
                device_id={"seq": lax.rem(me + hop, n)},
                device_id_type=MESH,
            )
            for which, (source, target) in enumerate(((send_k, recv_k), (send_v, recv_v)))
        ]

    bulk = [copy for pair in range((HOPS - 1) * CAP) for copy in block_copies(pair)]

    def send_blocks(turn):
        for copy in bulk[sum(TURNS[:turn]) : sum(TURNS[: turn + 1])]:
            copy.start()

    metas = [
        pltpu.make_async_remote_copy(
            src_ref=meta.at[hop],
            dst_ref=recv_meta.at[hop],
            send_sem=meta_sem.at[0, hop],
            recv_sem=meta_sem.at[1, hop],
            device_id={"seq": lax.rem(me + hop, n)},
            device_id_type=MESH,
        )
        for hop in range(1, HOPS)
    ]

    sq_start, sq_wait, sq_done = exchange(0, lambda d: sq_buf.at[me], sq_buf)
    sq_start()
    for copy in metas:
        copy.start()
    send_blocks(0)
    recv_meta[0] = meta[0]

    load_k.wait()
    load_v.wait()
    line = lax.broadcasted_iota(jnp.int32, (8, ROWS), 0)

    def in_groups(body):
        group = GROUP if n_blocks % GROUP == 0 else 1

        def some(i, carry):
            for j in range(group):
                body(i * group + j)
            return carry

        lax.fori_loop(0, n_blocks // group, some, 0)

    def fold(g):
        weights = fold_w[pl.ds(g, 1), :]
        high = weights.astype(BF16).astype(F32)
        rest = weights - high
        middle = rest.astype(BF16).astype(F32)
        low = rest - middle
        stacked = jnp.where(
            line == 0, high, jnp.where(line == 1, middle, jnp.where(line == 2, low, 0.0))
        ).astype(BF16)
        total = jnp.sum(weights, axis=1, keepdims=True)
        folded_k = jnp.dot(stacked, kbuf[g], preferred_element_type=F32)
        folded_v = jnp.dot(stacked, vbuf[g], preferred_element_type=F32)
        fk[pl.ds(g, 1), :] = (
            (jnp.sum(folded_k, axis=0, keepdims=True) / total).astype(BF16).astype(F32)
        )
        fv[pl.ds(g, 1), :] = (
            (jnp.sum(folded_v, axis=0, keepdims=True) / total).astype(BF16).astype(F32)
        )

    in_groups(fold)
    out_fk[...] = jnp.where(keep[...] > 0.5, 0.0, fk[...]).astype(BF16)
    out_fv[...] = jnp.where(keep[...] > 0.5, 0.0, fv[...]).astype(BF16)

    sq_wait()
    row = jnp.sum(sq_buf[...], axis=0)[0:1, :]
    col = jnp.sum(jnp.where(eye, row, 0.0), axis=1, keepdims=True)
    normed = (wide * lax.rsqrt(col / D + NORM_EPSILON)).astype(BF16)
    for part in range(3):
        product = jnp.dot(normed, w_qkv[part], preferred_element_type=F32)
        for d in range(n):
            part_send[d, part] = product[d * each : (d + 1) * each]
    part_start, part_wait, part_done = exchange(1, lambda d: part_send.at[d], part_recv)
    part_start()
    send_blocks(1)
    part_recv[me] = part_send[me]
    part_wait()
    proj = [jnp.sum(part_recv[:, part], axis=0) for part in range(3)]

    lane = lax.broadcasted_iota(jnp.int32, (each, width), 1)
    lower = lax.rem(lane, HDIM) < HDIM // 2
    my_cos, my_sin = cos[me], sin[me]

    def rotated(x):
        ahead = jnp.concatenate([x[:, HDIM // 2 :], x[:, : HDIM // 2]], axis=1)
        behind = jnp.concatenate([x[:, -(HDIM // 2) :], x[:, : -(HDIM // 2)]], axis=1)
        return (x * my_cos + jnp.where(lower, ahead, behind) * my_sin).astype(BF16).astype(F32)

    query = rotated(proj[0])
    new_key = rotated(proj[1])
    new_value = proj[2].astype(BF16).astype(F32)
    q_all[me] = query
    q_start, q_wait, q_done = exchange(2, lambda d: q_all.at[me], q_all)
    q_start()
    send_blocks(2)
    q_wait()

    q_rows = rows_of(q_all, n, each).astype(BF16)
    accs[...] = jnp.dot(onehot[...].astype(BF16), q_rows, preferred_element_type=F32)
    head_mask = (
        lax.broadcasted_iota(jnp.int32, (heads_here, width), 1) // HDIM
        == lax.broadcasted_iota(jnp.int32, (heads_here, width), 0)
    )

    def spread(column):
        return jnp.sum(jnp.where(head_mask, column, 0.0), axis=0, keepdims=True)

    def attend(g):
        query_g = jnp.where(head_mask, accs[pl.ds(g, 1), :], 0.0)
        scores = (
            lax.dot_general(
                query_g.astype(BF16),
                kbuf[g],
                (((1,), (1,)), ((), ())),
                preferred_element_type=F32,
            )
            * 0.125
        )
        top = jnp.max(scores, axis=1, keepdims=True)
        expo = jnp.exp(scores - top)
        total = jnp.sum(expo, axis=1, keepdims=True)
        mix = jnp.dot(expo.astype(BF16), vbuf[g], preferred_element_type=F32)
        mix = jnp.sum(jnp.where(head_mask, mix, 0.0), axis=0, keepdims=True)
        folded_score = jnp.sum(
            query_g * fk[pl.ds(g, 1), :], axis=1, keepdims=True
        ) * 0.125 + math.log(ROWS)
        kept = keep[pl.ds(g, 1), :] > 0.5
        tops[pl.ds(g, 1), :] = jnp.where(kept, spread(top), spread(folded_score))
        sums[pl.ds(g, 1), :] = jnp.where(kept, spread(total), 1.0)
        accs[pl.ds(g, 1), :] = jnp.where(kept, mix, fv[pl.ds(g, 1), :])

    in_groups(attend)
    block_tops = tops[...]
    req_top = jnp.full_like(block_tops, MASKED_SCORE)
    for g in range(n_blocks):
        req_top = jnp.maximum(
            req_top, jnp.where(same[:, g : g + 1] > 0.5, block_tops[g : g + 1], MASKED_SCORE)
        )
    factor = jnp.exp(block_tops - req_top)

    def by_request(table, array):
        return jnp.dot(table[...], array, precision=HIGHEST, preferred_element_type=F32)

    stat_lane = lax.broadcasted_iota(jnp.int32, (width, 128), 1)
    stat_row = lax.broadcasted_iota(jnp.int32, (width, 128), 0)
    pick_head = (stat_row == stat_lane * HDIM).astype(F32)
    sum_head = (stat_row // HDIM == stat_lane).astype(F32)

    def exact(left, right):
        return jnp.dot(left, right, precision=HIGHEST, preferred_element_type=F32)

    present = jnp.sum(first_t[...], axis=1, keepdims=True)
    top_rows = by_request(first_t, exact(req_top, pick_head))
    top_rows = jnp.where(present > 0.5, top_rows, MASKED_SCORE)
    sum_rows = by_request(onehot_t, exact(sums[...] * factor, pick_head))
    acc_rows = by_request(onehot_t, accs[...] * factor)
    for d in range(n):
        own_rows = slice(d * each, (d + 1) * each)
        mix_send[d, :, :width] = acc_rows[own_rows]
        mix_send[d, :, width : width + 128] = top_rows[own_rows]
        mix_send[d, :, width + 128 :] = sum_rows[own_rows]
    mix_start, mix_wait, mix_done = exchange(3, lambda d: mix_send.at[d], mix_recv)
    mix_start()
    send_blocks(3)
    mix_recv[me] = mix_send[me]

    spread_head = (
        lax.broadcasted_iota(jnp.int32, (128, width), 1) // HDIM
        == lax.broadcasted_iota(jnp.int32, (128, width), 0)
    ).astype(F32)
    own_score = exact(query * new_key, sum_head) * 0.125
    mix_wait()
    all_tops = mix_recv[:, :, width : width + 128]
    final_top = jnp.maximum(jnp.max(all_tops, axis=0), own_score)
    scale = jnp.exp(all_tops - final_top[None])
    own_expo = jnp.exp(own_score - final_top)
    totals = jnp.sum(mix_recv[:, :, width + 128 :] * scale, axis=0) + own_expo
    own_prob = own_expo.astype(BF16).astype(F32)
    mixture = exact(own_prob, spread_head) * new_value
    if each % 8 == 0:
        wide_scale = exact(scale.reshape(n * each, 128), spread_head).reshape(n, each, width)
        mixture = mixture + jnp.sum(mix_recv[:, :, :width] * wide_scale, axis=0)
    else:
        for d in range(n):
            mixture = mixture + mix_recv[d, :, :width] * exact(scale[d], spread_head)
    mixed_all[me] = (mixture / exact(totals, spread_head)).astype(BF16).astype(F32)
    mixed_start, mixed_wait, mixed_done = exchange(4, lambda d: mixed_all.at[me], mixed_all)
    mixed_start()
    send_blocks(4)
    mixed_wait()

    mixed_rows = rows_of(mixed_all, n, each).astype(BF16)
    head_buf[my_head] = jnp.dot(mixed_rows, w_out[...], preferred_element_type=F32)
    head_copies = [
        pltpu.make_async_remote_copy(
            src_ref=head_buf.at[my_head],
            dst_ref=head_buf.at[my_head],
            send_sem=head_sem.at[0, k],
            recv_sem=head_sem.at[1, k],
            device_id={"heads": lax.rem(my_head + k, n_heads)},
            device_id_type=MESH,
        )
        for k in range(1, n_heads)
    ]
    for copy in head_copies:
        copy.start()
    send_blocks(5)
    for copy in head_copies:
        copy.wait_recv()
    total = head_buf[0]
    for h in range(1, n_heads):
        total = total + head_buf[h]
    out_attn[...] = total.astype(BF16)

    for done in (sq_done, part_done, q_done, mix_done, mixed_done):
        done()
    for copy in head_copies:
        copy.wait_send()
    for copy in metas + bulk:
        copy.wait()


def shards(
    n,
    n_heads,
    hidden,
    w_qkv,
    w_out,
    positions,
    req_blocks,
    keep_list,
    dest_slot,
    key_cache,
    value_cache,
    fold_weight,
):
    requests = hidden.shape[0]
    n_blocks, row_count, width = key_cache.shape
    me = lax.axis_index("seq")
    each = requests // n
    moved = (HOPS - 1) * CAP

    ids = jnp.arange(requests, dtype=jnp.int32)
    ends = jnp.sum(jnp.where(ids[None, :] <= ids[:, None], req_blocks[None, :], 0), axis=1)
    block_ids = jnp.arange(n_blocks, dtype=jnp.int32)
    global_ids = me * n_blocks + block_ids
    blk_req = jnp.sum((global_ids[:, None] >= ends[None, :]).astype(jnp.int32), axis=1)
    onehot = (blk_req[:, None] == ids[None, :]).astype(F32)
    onehot_t = (blk_req[None, :] == ids[:, None]).astype(F32)
    same_bool = blk_req[:, None] == blk_req[None, :]
    same = same_bool.astype(F32)
    has_earlier = jnp.any(same_bool & (block_ids[None, :] < block_ids[:, None]), axis=1)
    first_t = jnp.where(has_earlier[None, :], 0.0, onehot_t)
    keep_rows = jnp.broadcast_to((keep_list == 1).astype(F32)[:, None], (n_blocks, width))

    half = HDIM // 2
    freqs = ROPE_BASE ** (-(2.0 * jnp.arange(half, dtype=F32)) / HDIM)
    angles = positions.astype(F32)[:, None] * freqs[None, :]
    cos_half, sin_half = jnp.cos(angles), jnp.sin(angles)
    copies = width // HDIM
    cos = jnp.tile(jnp.concatenate([cos_half, cos_half], axis=1), (1, copies))
    sin = jnp.tile(jnp.concatenate([-sin_half, sin_half], axis=1), (1, copies))
    cos = cos.reshape(n, each, width)
    sin = sin.reshape(n, each, width)

    smem = pl.BlockSpec(memory_space=pltpu.SMEM)
    vmem = pl.BlockSpec(memory_space=pltpu.VMEM)
    hbm = pl.BlockSpec(memory_space=pl.ANY)
    moved_shape = jax.ShapeDtypeStruct((moved, row_count, width), BF16)
    own_shape = jax.ShapeDtypeStruct((CAP, row_count, width), BF16)
    meta_shape = jax.ShapeDtypeStruct((HOPS, 8, 128), jnp.int32)
    folded_shape = jax.ShapeDtypeStruct((n_blocks, width), BF16)

    own_k, own_v, send_k, send_v, meta = pl.pallas_call(
        functools.partial(pack_kernel, n),
        out_shape=(own_shape, own_shape, moved_shape, moved_shape, meta_shape),
        in_specs=[smem, smem, smem, vmem, vmem],
        out_specs=(vmem, vmem, vmem, vmem, smem),
        scratch_shapes=[pltpu.SMEM((HOPS,), jnp.int32)],
        compiler_params=pltpu.CompilerParams(vmem_limit_bytes=32 * 2**20),
        name="pack_blocks",
    )(keep_list, dest_slot, blk_req, key_cache, value_cache)

    block_rows = pltpu.VMEM((n_blocks, width), F32)
    request_rows = pltpu.VMEM((n, each, width), F32)
    partials = pltpu.VMEM((n, each, width + 256), F32)
    three_parts = pltpu.VMEM((n, 3, each, width), F32)
    recv_k, recv_v, recv_meta, folded_keys, folded_values, attn_out = pl.pallas_call(
        functools.partial(main_kernel, n, n_heads),
        out_shape=(
            moved_shape,
            moved_shape,
            meta_shape,
            folded_shape,
            folded_shape,
            jax.ShapeDtypeStruct((requests, w_out.shape[1]), BF16),
        ),
        in_specs=[vmem] * 12 + [hbm] * 4,
        out_specs=(hbm, hbm, vmem, vmem, vmem, vmem),
        scratch_shapes=[
            pltpu.VMEM((n_blocks, row_count, width), BF16),
            pltpu.VMEM((n_blocks, row_count, width), BF16),
            block_rows,
            block_rows,
            block_rows,
            block_rows,
            block_rows,
            pltpu.VMEM((n, 8, 128), F32),
            three_parts,
            three_parts,
            request_rows,
            partials,
            partials,
            request_rows,
            pltpu.VMEM((n_heads, requests, w_out.shape[1]), F32),
            pltpu.SemaphoreType.DMA((2,)),
            pltpu.SemaphoreType.DMA((4, (HOPS - 1) * CAP)),
            pltpu.SemaphoreType.DMA((2, HOPS)),
            pltpu.SemaphoreType.DMA((10, n)),
            pltpu.SemaphoreType.DMA((2, n_heads)),
        ],
        compiler_params=pltpu.CompilerParams(
            collective_id=0, has_side_effects=True, vmem_limit_bytes=48 * 2**20
        ),
        name="decode_and_move",
    )(
        hidden,
        jnp.transpose(w_qkv, (1, 0, 2)),
        w_out,
        cos,
        sin,
        onehot,
        onehot_t,
        first_t,
        same,
        keep_rows,
        fold_weight,
        meta,
        key_cache,
        value_cache,
        send_k,
        send_v,
    )

    packed_shape = jax.ShapeDtypeStruct((SLOT_DEV, row_count, width), BF16)
    packed_keys, packed_values, packed_request = pl.pallas_call(
        place_kernel,
        out_shape=(packed_shape, packed_shape, jax.ShapeDtypeStruct((SLOT_DEV,), jnp.int32)),
        in_specs=[smem, vmem, vmem, vmem, vmem],
        out_specs=(hbm, hbm, smem),
        scratch_shapes=[pltpu.VMEM((row_count, width), BF16), pltpu.SemaphoreType.DMA],
        compiler_params=pltpu.CompilerParams(vmem_limit_bytes=32 * 2**20),
        name="place_blocks",
    )(recv_meta, own_k, own_v, recv_k, recv_v)
    return (packed_keys, packed_values, packed_request, folded_keys, folded_values, attn_out)


def solution(mesh):
    return jax.shard_map(
        functools.partial(shards, mesh.shape["seq"], mesh.shape["heads"]),
        mesh=mesh,
        in_specs=(
            P(None, "seq"),
            P("seq", None, "heads"),
            P("heads", "seq"),
            P(),
            P(),
            P("seq"),
            P("seq"),
            P("seq", None, "heads"),
            P("seq", None, "heads"),
            P("seq", None),
        ),
        out_specs=(
            P("seq", None, "heads"),
            P("seq", None, "heads"),
            P("seq"),
            P("seq", "heads"),
            P("seq", "heads"),
            P(None, "seq"),
        ),
        check_vma=False,
    )
```
